32 devices in a mesh: expert: 8 (over z, core), tensor: 4 (over y, x).
Axes of the slice: x: 2, y: 2, z: 4, core: 2. Of those that a mesh axis runs over, the one named last changes fastest.
Arguments:
- hidden_in: bfloat16 [1024, 4096], P('expert', 'tensor'), may hold values from -92 to 92
- norm_gain: float32 [4096], P('tensor'), may hold values from 0.5 to 1.5
- expert_ids: int32 [1024, 8], P('expert'), may hold values from 0 to 15, all different within a row; in each aligned block of 128 rows (0 to 127, 128 to 255, ...) at most 96 rows name the same one
- route_weights: float32 [1024, 8], P('expert'), may hold values from 0.05 to 0.5
- w_gate: bfloat16 [16, 1536, 4096], P('expert', 'tensor'), may hold values from -0.09375 to 0.09375
- w_up: bfloat16 [16, 1536, 4096], P('expert', 'tensor'), may hold values from -0.09375 to 0.09375
- w_down: bfloat16 [16, 1536, 4096], P('expert', 'tensor'), may hold values from -0.15625 to 0.15625
Outputs:
- moe_out: bfloat16 [1024, 4096], P('expert', 'tensor')
The draws below stay inside these ranges and needn't reach their ends.
Inputs may be any that keep to these rules, and one draw needn't show every extreme that they name: `expert_ids`: in each aligned block of 128 rows (the rows of one index of the expert axis) no expert is named by more than 96 rows, a bound that some block reaches.
All inputs are finite; a program needn't handle non-finite values.
Results may differ from the reference program's by a relative error of at most 0.019.
Values may be sent and summed in bfloat16 or wider, within the bound.
No kernel may reach another device: no remote copies, remote signals or barrier semaphores. Data moves between devices by JAX's collectives and lax.ppermute only.
A program may use at most 128 MiB of HBM per device.

```python
import math
import jax
import jax.numpy as jnp
import numpy as np
from jax import lax

D = 4096
FF = 1536
TOPK = 8
TOK_DEV = 128
EXPERTS = 16
TOKENS = 1024
CAP = 96
N_EXPERT = 8
N_TENSOR = 4


def draw_hidden_in(key, part):
    first, second = jax.random.split(key, 2)
    column = jnp.arange(D, dtype=jnp.float32) / D
    level = jax.random.uniform(second, (TOKENS, 1), jnp.float32, 0.0, 1.0)
    base = jnp.clip(jax.random.normal(first, (TOKENS, D), jnp.float32), -4.0, 4.0)
    scale = 10.0 ** level * (3.0 ** column)[None, :] * 0.5
    return (base * scale).astype(jnp.bfloat16)


def steps_of(stream_key, dims, shards, smallest, largest):
    def one(dim, blocks):
        draws = jax.random.uniform(jax.random.fold_in(jax.random.fold_in(stream_key, 6), dim), (blocks,), jnp.float32, smallest / len(shards), largest / len(shards))
        return jnp.repeat(jnp.exp(draws), dims[dim] // blocks).reshape((-1,) + (1,) * (len(dims) - dim - 1))

    factor_of = one(*shards[0])
    for cut in shards[1:]:
        factor_of = factor_of * one(*cut)
    return factor_of


def assign_block(rng, own, number, rows, amount, top, most, lean):
    sequence = jax.random.permutation(rng, amount)
    crowded, usual = portions_of(amount, rows * top, most, lean, True), portions_of(amount, rows * top, most, lean, False)
    places = jnp.arange(amount)

    def named(tallies, offset_by):
        used = int((tallies > 0).sum())
        fixed = max(1, used // 4)
        shifted = fixed + (places - fixed + offset_by * (used - fixed)) % max(1, amount - fixed)
        return jnp.zeros((amount,), jnp.int32).at[sequence[jnp.where(places < fixed, places, shifted)]].set(jnp.asarray(tallies, jnp.int32))

    tallies = jnp.where(number % 4 == 0, named(crowded, number // 4), named(usual, number - number // 4 - 1))
    mixed = jax.random.permutation(jax.random.fold_in(own, 3), amount)
    source_of, taker = mixed[0:amount // 2 * 2:2], mixed[1:amount // 2 * 2:2]
    slack = jnp.minimum(tallies[source_of] - 1, most - tallies[taker]) // 2
    slack = jnp.where((source_of == sequence[0]) | (taker == sequence[0]) | (tallies[taker] == 0), 0, jnp.maximum(slack, 0))
    shifted = jax.random.randint(jax.random.fold_in(own, 4), (amount // 2,), 0, 1 << 20) % (slack + 1)
    tallies = tallies.at[source_of].add(-shifted).at[taker].add(shifted)
    items = jnp.searchsorted(jnp.cumsum(tallies), jnp.arange(rows * top), side="right").astype(jnp.int32)
    table = items.reshape(top, rows).T
    table = table[jax.random.permutation(jax.random.fold_in(own, 1), rows)]
    offset_by = jax.random.randint(jax.random.fold_in(own, 2), (rows, 1), 0, top)
    return jnp.take_along_axis(table, (jnp.arange(top)[None, :] + offset_by) % top, axis=1)


def portions_of(amount, total, reach, lean, full):
    loads = [(1 << 20) // math.isqrt(standing ** lean) + 1 for standing in range(1, amount + 1)]
    largest = reach if full else min(reach, max(-(-total // amount), total * loads[0] // sum(loads)))
    least = 1 if total - largest >= amount - 1 else 0
    given, rest = [largest] + [least] * (amount - 1), total - largest - least * (amount - 1)
    while rest > 0:
        movable = [i for i in range(1, amount) if given[i] < largest] or [i for i in range(1, amount) if given[i] < reach]
        whole, remaining = sum([loads[i] for i in movable]), rest
        for i in movable:
            addition = min(reach - given[i], max(1, remaining * loads[i] // whole), rest)
            given[i] = given[i] + addition
            rest = rest - addition
    return np.array(given)


def centred(stream_key, dims, width, bound, shards=(), held_as=jnp.bfloat16):
    values = width * jax.random.normal(stream_key, dims, jnp.float32)
    if shards:
        values = values * steps_of(stream_key, dims, shards, -0.22, 0.18)
    return jnp.clip(values, -bound, bound).astype(held_as)


def setup_inputs(seed: int = 0) -> dict:
    key_list = jax.random.split(jax.random.key(seed), 8)
    hidden_in = draw_hidden_in(jax.random.fold_in(key_list[7], 71), 0)
    norm_gain = jnp.clip(1.0 + 0.1 * jax.random.normal(key_list[1], (D,), jnp.float32), 0.5, 1.5)
    expert_ids_keys = jax.random.split(jax.random.fold_in(key_list[2], 1), TOKENS // TOK_DEV)
    expert_ids_turns = jax.random.permutation(jax.random.fold_in(key_list[2], 3), TOKENS // TOK_DEV)
    expert_ids = jax.vmap(lambda own, number: assign_block(jax.random.fold_in(key_list[2], 2), own, number, TOK_DEV, EXPERTS, TOPK, CAP, 2))(expert_ids_keys, expert_ids_turns).reshape((TOKENS, TOPK))
    route_weights = jnp.clip(jnp.exp(math.log(0.5) - 2.3025851 * jax.random.uniform(key_list[3], (TOKENS, TOPK), jnp.float32) ** steps_of(key_list[3], (TOKENS, TOPK), ((0, 8),), -0.2, 0.2)), 0.05, 0.5)
    w_gate = centred(key_list[4], (EXPERTS, FF, D), D ** -0.5, 0.09375, ((0, 8), (1, 4)))
    w_up = centred(key_list[5], (EXPERTS, FF, D), D ** -0.5, 0.09375, ((0, 8), (1, 4)))
    w_down = centred(key_list[6], (EXPERTS, FF, D), FF ** -0.5, 0.15625, ((0, 8), (1, 4)))
    return dict(hidden_in=hidden_in, norm_gain=norm_gain, expert_ids=expert_ids, route_weights=route_weights, w_gate=w_gate, w_up=w_up, w_down=w_down)


epsilon = 1e-06

def reference(hidden_in, norm_gain, expert_ids, route_weights, w_gate, w_up, w_down):
    widened = hidden_in.astype(jnp.float32)
    squares = lax.optimization_barrier(jnp.sum(widened * widened, axis=1, keepdims=True))
    normed = (widened * lax.rsqrt(squares / D + epsilon) * norm_gain[None, :]).astype(jnp.bfloat16)
    blocks = expert_ids.reshape(N_EXPERT, TOK_DEV, TOPK)
    picked_mask = (blocks[:, :, :, None] == jnp.arange(EXPERTS, dtype=jnp.int32)[None, None, None, :]).astype(jnp.int32)
    chosen = lax.optimization_barrier(jnp.sum(picked_mask, axis=2))
    before = jnp.cumsum(chosen, axis=1) - chosen
    position = lax.optimization_barrier(jnp.sum(picked_mask * before[:, :, None, :], axis=3))
    source = jnp.arange(N_EXPERT, dtype=jnp.int32)[:, None, None]
    row_index = ((blocks * N_EXPERT + source) * CAP + position).reshape(TOKENS * TOPK).astype(jnp.int32)
    spread_rows = jnp.repeat(normed, TOPK, axis=0)
    dense = jnp.zeros((EXPERTS * N_EXPERT * CAP, D), jnp.bfloat16).at[row_index].set(spread_rows)
    dense = dense.reshape(EXPERTS, N_EXPERT * CAP, D)
    group = FF // N_TENSOR
    contract = (((1,), (1,)), ((), ()))

    def one_expert(operands):
        rows, gate_w, up_w, down_w = operands
        gate = lax.dot_general(rows, gate_w, contract, preferred_element_type=jnp.float32)
        up_val = lax.dot_general(rows, up_w, contract, preferred_element_type=jnp.float32)
        inner = (jax.nn.silu(gate) * up_val).astype(jnp.bfloat16)
        split_inner = inner.reshape(rows.shape[0], N_TENSOR, group).astype(jnp.float32)
        split_down = down_w.reshape(N_TENSOR, group, D).astype(jnp.float32)
        parts = jnp.einsum('rgf,gfd->grd', split_inner, split_down)
        rounded = lax.optimization_barrier(parts.astype(jnp.bfloat16))
        return lax.optimization_barrier(jnp.sum(rounded.astype(jnp.float32), axis=0))
    outputs = lax.map(one_expert, (dense, w_gate, w_up, w_down))
    lookup = outputs.reshape(EXPERTS * N_EXPERT * CAP, D)
    gathered = lookup[row_index].reshape(TOKENS, TOPK, D)
    mixed = lax.optimization_barrier(jnp.sum(gathered * route_weights[:, :, None], axis=1))
    return mixed.astype(jnp.bfloat16)
```

```python
import functools

import jax
import jax.numpy as jnp
from jax import lax
from jax.experimental import pallas as pl
from jax.experimental.pallas import tpu as pltpu
from jax.sharding import PartitionSpec as P

AXES = ("expert", "tensor")
CORES = 2
EXTRA = 8
epsilon = 1e-06
NT = (((1,), (1,)), ((), ()))


def split3(v):
    hi = v.astype(jnp.bfloat16)
    rest = v - hi.astype(jnp.float32)
    mid = rest.astype(jnp.bfloat16)
    lo = (rest - mid.astype(jnp.float32)).astype(jnp.bfloat16)
    return hi, mid, lo


def masks_of(n_tensor):
    bits = n_tensor.bit_length() - 1
    first = [1 << b for b in range(bits)]
    half = bits // 2
    return first, first[half:] + first[:half]


def spread(masks, j):
    out = 0
    for s, m in enumerate(masks):
        if (j >> s) & 1:
            out ^= m
    return out


def expert_kernel(pieces, offsets, block, order_ref, *refs):
    n_in = 2 * 2
    (a0, a1, b0, b1, scal, wg, wu, wd) = refs[: n_in + 4]
    (mine_keep, mine_send, sib_keep, sib_send) = refs[n_in + 4 : n_in + 8]
    xs, hs = refs[n_in + 8 :]
    half = pieces // 2
    rows = offsets * block
    width = xs.shape[2]
    for side, (lo, hi) in enumerate(((a0, a1), (b0, b1))):
        for j in range(pieces):
            src = lo if j < half else hi
            q = order_ref[side, j]
            for o in range(offsets):
                at = side * rows + o * block
                xs[q, at : at + block, :] = src[j % half, o, 0:block, :]
    n_exp, hidden = wg.shape[0], wg.shape[1]
    scale = scal[:, 0:1]
    for e in range(n_exp):
        gate = jnp.zeros((2 * rows, hidden), jnp.float32)
        up = jnp.zeros((2 * rows, hidden), jnp.float32)
        for q in range(pieces):
            cols = slice(q * width, (q + 1) * width)
            gate += lax.dot_general(xs[q], wg[e, :, cols], NT, preferred_element_type=jnp.float32)
            up += lax.dot_general(xs[q], wu[e, :, cols], NT, preferred_element_type=jnp.float32)
        gate = gate * scale
        inner = gate / (1.0 + jnp.exp(-gate)) * (up * scale) * scal[:, 1 + e : 2 + e]
        hs[:, e * hidden : (e + 1) * hidden] = inner.astype(jnp.bfloat16)
    for side, (keep, send) in enumerate(((mine_keep, mine_send), (sib_keep, sib_send))):
        inner = hs[side * rows : (side + 1) * rows, :]
        for j in range(pieces):
            q = order_ref[side, j]
            cols = pl.ds(pl.multiple_of(q * width, width), width)
            out = jnp.dot(inner, wd[:, cols], preferred_element_type=jnp.float32)
            dst = keep if j < half else send
            for o in range(offsets):
                dst[j % half, o] = out[o * block : (o + 1) * block].astype(jnp.bfloat16)


def run_experts(order, a0, a1, b0, b1, scal, wg, wu, wd, block):
    half, offsets, _, width = a0.shape
    pieces = 2 * half
    rows = offsets * block
    hidden = wg.shape[0] * wg.shape[1]
    part = jax.ShapeDtypeStruct((half, offsets, block, width), jnp.bfloat16)
    vmem = pl.BlockSpec(memory_space=pltpu.VMEM)
    macs = 2 * rows * 3 * hidden * pieces * width
    return pl.pallas_call(
        functools.partial(expert_kernel, pieces, offsets, block),
        out_shape=[part] * 4,
        in_specs=[pl.BlockSpec(memory_space=pltpu.SMEM)] + [vmem] * 8,
        out_specs=[vmem] * 4,
        scratch_shapes=[
            pltpu.VMEM((pieces, 2 * rows, width), jnp.bfloat16),
            pltpu.VMEM((2 * rows, hidden), jnp.bfloat16),
        ],
        compiler_params=pltpu.CompilerParams(vmem_limit_bytes=56 * 1024 * 1024),
        cost_estimate=pl.CostEstimate(
            flops=2 * macs, bytes_accessed=3 * hidden * pieces * width * 2, transcendentals=2 * rows * hidden
        ),
    )(order, a0, a1, b0, b1, scal, wg, wu, wd)


def body(hidden_in, norm_gain, expert_ids, route_weights, w_gate, w_up, w_down):
    block, width = hidden_in.shape
    exp_local = w_gate.shape[0]
    groups, n_tensor = lax.axis_size("expert"), lax.axis_size("tensor")
    n_z = groups // CORES
    experts_all = exp_local * groups
    group_here, slice_here = lax.axis_index("expert"), lax.axis_index("tensor")
    core = group_here % CORES
    masks = masks_of(n_tensor)
    stages = len(masks[0])

    def send(value, target):
        pairs = []
        for z in range(n_z):
            for c in range(CORES):
                for t in range(n_tensor):
                    z2, c2, t2 = target(z, c, t)
                    pairs.append(((z * CORES + c) * n_tensor + t, (z2 * CORES + c2) * n_tensor + t2))
        return lax.ppermute(value, AXES, pairs)

    def stage_swap(value, s):
        return send(value, lambda z, c, t: (z, c, t ^ masks[c][s]))

    def core_swap(value):
        return send(value, lambda z, c, t: (z, 1 - c, t))

    widened = hidden_in.astype(jnp.float32)
    scaled = (widened * norm_gain[None, :]).astype(jnp.bfloat16)
    squares = jnp.sum(widened * widened, axis=1)
    dense = jnp.sum(
        jnp.where(
            expert_ids.T[None, :, :] == jnp.arange(experts_all, dtype=jnp.int32)[:, None, None],
            route_weights.T[None, :, :],
            0.0,
        ),
        axis=1,
    )
    table = jnp.concatenate([squares[None, :], dense], axis=0)
    extra = jnp.stack(split3(table), axis=1).reshape(-1)
    n_extra = -(-extra.shape[0] // (EXTRA * width)) * EXTRA
    extra = jnp.pad(extra, (0, n_extra * width - extra.shape[0])).reshape(n_extra, width)
    payload = jnp.concatenate([scaled, extra], axis=0)

    chunk = [[spread(masks[c], j) for j in range(n_tensor)] for c in range(CORES)]
    order = slice_here ^ jnp.array([chunk, chunk[::-1]], jnp.int32)[core]

    near = [0]
    for k in range(1, n_z // 2 + 1):
        near += [k] if 2 * k == n_z else [k, n_z - k]
    plans = [[k] for k in near]

    arrived = [payload if k == 0 else send(payload, lambda z, c, t, k=k: ((z - k) % n_z, c, t)) for k in near]
    arrived = dict(zip(near, arrived))
    wd = w_down.reshape(-1, w_down.shape[2])
    total = None
    back = {}
    for plan in plans:
        blk = jnp.stack([arrived[k] for k in plan], axis=0)[None]
        for s in range(stages - 1):
            blk = jnp.concatenate([blk, stage_swap(blk, s)], axis=0)
        far = stage_swap(blk, stages - 1)
        blk_sib = core_swap(blk)
        far_sib = core_swap(far)

        def tables(lo, hi):
            both = jnp.concatenate([lo[:, :, block:], hi[:, :, block:]], axis=0).astype(jnp.float32)
            flat = both.reshape(n_tensor, len(plan), -1)[:, :, : 3 * (1 + experts_all) * block]
            flat = flat.reshape(n_tensor, len(plan), 1 + experts_all, 3, block)
            flat = flat[:, :, :, 0] + flat[:, :, :, 1] + flat[:, :, :, 2]
            total_squares = jnp.sum(flat[:, :, 0], axis=0)
            scale = lax.rsqrt(total_squares / (n_tensor * width) + epsilon)
            weights = lax.dynamic_slice_in_dim(flat[0], 1 + group_here * exp_local, exp_local, axis=1)
            return jnp.concatenate([scale[:, None], weights], axis=1).transpose(0, 2, 1).reshape(-1, 1 + exp_local)

        scal = jnp.concatenate([tables(blk, far), tables(blk_sib, far_sib)], axis=0)
        mine_keep, mine_send, sib_keep, sib_send = run_experts(
            order, blk, far, blk_sib, far_sib, scal, w_gate, w_up, wd, block
        )
        f32 = jnp.float32
        from_sib = core_swap(sib_send)
        out = (mine_send.astype(f32) + from_sib.astype(f32)).astype(jnp.bfloat16)
        keep = mine_keep.astype(f32) + core_swap(sib_keep).astype(f32)
        for s in range(stages - 1, -1, -1):
            got = stage_swap(out, s)
            keep = keep + got.astype(f32)
            if s:
                half = keep.shape[0] // 2
                out = keep[half:].astype(jnp.bfloat16)
                keep = keep[:half]
        done = keep[0]
        for i, k in enumerate(plan):
            if k == 0:
                back[k] = done[i]
            else:
                back[k] = send(
                    done[i].astype(jnp.bfloat16), lambda z, c, t, k=k: ((z + k) % n_z, c, t)
                ).astype(f32)
    total = back[near[0]]
    for k in near[1:]:
        total = total + back[k]
    return total.astype(jnp.bfloat16)


def solution(mesh):
    placed = (
        P("expert", "tensor"),
        P("tensor"),
        P("expert", None),
        P("expert", None),
        P("expert", "tensor", None),
        P("expert", "tensor", None),
        P("expert", "tensor", None),
    )
    return jax.shard_map(
        body, mesh=mesh, in_specs=placed, out_specs=P("expert", "tensor"), check_vma=False
    )
```

```python
import functools

import jax
import jax.numpy as jnp
from jax import lax
from jax.experimental import pallas as pl
from jax.experimental.pallas import tpu as pltpu
from jax.sharding import PartitionSpec as P

AXES = ("expert", "tensor")
CORES = 2
LANES = 128
SPLIT = 3
epsilon = 1e-06
NT = (((1,), (1,)), ((), ()))
TN = (((0,), (0,)), ((), ()))
f32 = jnp.float32
bf16 = jnp.bfloat16
VMEM = pl.BlockSpec(memory_space=pltpu.VMEM)
SMEM = pl.BlockSpec(memory_space=pltpu.SMEM)


def masks_of(n_tensor):
    first = [1 << b for b in range(n_tensor.bit_length() - 1)]
    return first, first[::-1]


def spread(masks, j):
    out = 0
    for s, m in enumerate(masks):
        if (j >> s) & 1:
            out ^= m
    return out


def mirror(pieces, j):
    first, second = masks_of(pieces)
    return spread([1 << second.index(m) for m in first], j)


def payload_kernel(experts_all, hidden, gain, ids, weights, out):
    block, width = hidden.shape
    h = hidden[...].astype(f32)
    out[0:block, :] = (h * gain[...]).astype(bf16)
    squares = jnp.sum(h * h, axis=1, keepdims=True)
    rows = [jnp.broadcast_to(squares, (block, LANES)).T[0:1, :]]
    for e in range(experts_all):
        rows.append(jnp.sum(jnp.where(ids[...] == e, weights[...], 0.0), axis=0, keepdims=True))
    slots = []
    for v in rows:
        for _ in range(SPLIT):
            part = v.astype(bf16).astype(f32)
            slots.append(part)
            v = v - part
    per_row = width // LANES
    zero = jnp.zeros((1, LANES), f32)
    n_extra = out.shape[0] - block
    slots += [zero] * (n_extra * per_row - len(slots))
    lines = [jnp.concatenate(slots[r * per_row : (r + 1) * per_row], axis=1) for r in range(n_extra)]
    out[block:, :] = jnp.concatenate(lines, axis=0).astype(bf16)


def expert_kernel(pieces, offsets, block, fetch, *refs):
    place, first, a0, a1, b0, b1, wg, wu, wd = refs[:9]
    mine_keep, mine_send, sib_keep, sib_send = refs[9:13]
    xs, hs = refs[13 + 3 * fetch : 15 + 3 * fetch]
    half = pieces // 2
    rows = offsets * block
    width = a0.shape[3]
    n_extra = a0.shape[2] - block
    n_exp, hidden = wg.shape[0], wg.shape[1]
    others = [mirror(pieces, j) for j in range(pieces)]

    def piece(side, j):
        j = others[j] if side else j
        return ((a0, a1), (b0, b1))[side][j // half], j % half

    def columns(j):
        return pl.ds(pl.multiple_of(place[j] * width, width), width)

    copies = []
    if fetch:
        (wg_from, wu_from, wd_from), (wg, wu, wd), sems = (wg, wu, wd), refs[13:16], refs[-1]
        moves = [(x.at[e], y.at[e]) for e in range(n_exp) for x, y in ((wg_from, wg), (wu_from, wu))]
        moves += [(wd_from.at[:, columns(j)], wd.at[:, columns(j)]) for j in range(pieces)]
        copies = [pltpu.make_async_copy(x, y, sems.at[n]) for n, (x, y) in enumerate(moves)]
        for copy in copies:
            copy.start()

    def wait(n):
        if copies:
            copies[n].wait()

    for side in range(2):
        for j in range(pieces):
            src, i = piece(side, j)
            for o in range(offsets):
                at = side * rows + o * block
                xs[at : at + block, j * width : (j + 1) * width] = src[i, o, 0:block, :]

    value = (
        lax.broadcasted_iota(jnp.int32, (n_extra, width), 0) * (width // LANES)
        + lax.broadcasted_iota(jnp.int32, (n_extra, width), 1) // LANES
    ) // SPLIT

    def pick(table, v):
        row = jnp.sum(jnp.where(value == v, table, 0.0), axis=0, keepdims=True)
        return sum(row[:, g * LANES : (g + 1) * LANES] for g in range(width // LANES))

    scales, picked = [], [[] for _ in range(n_exp)]
    for side in range(2):
        for o in range(offsets):
            tables = []
            for j in range(pieces):
                src, i = piece(side, j)
                tables.append(src[i, o, block:, :].astype(f32))
            scales.append(pick(sum(tables), 0))
            for e in range(n_exp):
                picked[e].append(pick(tables[0], first[0] + (1 + e)))
    scale = lax.rsqrt(jnp.concatenate(scales, axis=1) / (pieces * width) + epsilon)

    for e in range(n_exp):
        wait(2 * e)
        wait(2 * e + 1)
        gate = jnp.zeros((hidden, 2 * rows), f32)
        up = jnp.zeros((hidden, 2 * rows), f32)
        for j in range(pieces):
            x = xs[:, j * width : (j + 1) * width]
            gate += lax.dot_general(wg[e, :, columns(j)], x, NT, preferred_element_type=f32)
            up += lax.dot_general(wu[e, :, columns(j)], x, NT, preferred_element_type=f32)
        gate = gate * scale
        inner = gate / (1.0 + jnp.exp(-gate)) * (up * scale) * jnp.concatenate(picked[e], axis=1)
        hs[e * hidden : (e + 1) * hidden, :] = inner.astype(bf16)

    for j in range(pieces):
        wait(2 * n_exp + j)
        out = lax.dot_general(hs[...], wd[:, columns(j)], TN, preferred_element_type=f32).astype(bf16)
        for side, (keep, away) in enumerate(((mine_keep, mine_send), (sib_keep, sib_send))):
            to = others[j] if side else j
            for o in range(offsets):
                at = side * rows + o * block
                (keep if to < half else away)[to % half, o] = out[at : at + block]


def run_experts(place, first, a0, a1, b0, b1, weights, block, fetch):
    half, offsets, _, width = a0.shape
    pieces = 2 * half
    rows = offsets * block
    n_exp, hidden = weights[0].shape[0], weights[2].shape[0]
    held = [pltpu.VMEM(w.shape, w.dtype) for w in weights] if fetch else []
    sems = [pltpu.SemaphoreType.DMA((2 * n_exp + pieces,))] if fetch else []
    out = pl.pallas_call(
        functools.partial(expert_kernel, pieces, offsets, block, fetch),
        out_shape=[jax.ShapeDtypeStruct((half, offsets, block, width), bf16)] * 4 + held,
        in_specs=[SMEM] * 2 + [VMEM] * 4 + [pl.BlockSpec(memory_space=pl.ANY) if fetch else VMEM] * 3,
        out_specs=[VMEM] * (4 + len(held)),
        scratch_shapes=[
            pltpu.VMEM((2 * rows, pieces * width), bf16),
            pltpu.VMEM((hidden, 2 * rows), bf16),
        ]
        + sems,
        compiler_params=pltpu.CompilerParams(vmem_limit_bytes=30 * 1024 * 1024),
        cost_estimate=pl.CostEstimate(
            flops=4 * rows * 3 * hidden * pieces * width,
            bytes_accessed=8 * rows * pieces * width,
            transcendentals=2 * rows * hidden,
        ),
    )(place, first, a0, a1, b0, b1, *weights)
    if fetch:
        weights = [pltpu.with_memory_space_constraint(w, pltpu.VMEM) for w in out[4:]]
    return out[:4], weights


def body(hidden_in, norm_gain, expert_ids, route_weights, w_gate, w_up, w_down):
    block, width = hidden_in.shape
    exp_local = w_gate.shape[0]
    groups, n_tensor = lax.axis_size("expert"), lax.axis_size("tensor")
    n_z = groups // CORES
    experts_all = exp_local * groups
    group_here, slice_here = lax.axis_index("expert"), lax.axis_index("tensor")
    core = group_here % CORES
    masks = masks_of(n_tensor)
    stages = len(masks[0])

    def send(value, target):
        pairs = []
        for z in range(n_z):
            for c in range(CORES):
                for t in range(n_tensor):
                    z2, c2, t2 = target(z, c, t)
                    pairs.append(((z * CORES + c) * n_tensor + t, (z2 * CORES + c2) * n_tensor + t2))
        return lax.ppermute(value, AXES, pairs)

    def stage_swap(value, s):
        return send(value, lambda z, c, t: (z, c, t ^ masks[c][s]))

    def core_swap(value):
        return send(value, lambda z, c, t: (z, 1 - c, t))

    def shift(value, k):
        return send(value, lambda z, c, t: ((z + k) % n_z, c, t)) if k % n_z else value

    slots = SPLIT * (1 + experts_all)
    n_extra = -(-slots // (8 * width // LANES)) * 8
    payload = pl.pallas_call(
        functools.partial(payload_kernel, experts_all),
        out_shape=jax.ShapeDtypeStruct((block + n_extra, width), bf16),
        in_specs=[VMEM] * 4,
        out_specs=VMEM,
    )(hidden_in, norm_gain[None, :], expert_ids.T, route_weights.T)

    chunk = [[spread(masks[c], j) for j in range(n_tensor)] for c in range(CORES)]
    place = slice_here ^ jnp.array(chunk, jnp.int32)[core]
    first = (group_here * exp_local).astype(jnp.int32)[None]

    weights = [w_gate, w_up, w_down.reshape(-1, w_down.shape[2])]

    near = sorted(range(n_z), key=lambda k: min(k, n_z - k))
    blk, far, blk_sib, out, keep, back = {0: payload[None, None]}, {}, {}, {}, {}, {}
    tied = range(1, n_z + 2 * stages)

    def put(store, i, value):
        store[i] = value

    def summed(i, s, got):
        kept = keep[i] + got.astype(f32)
        half = kept.shape[0] // 2
        if s:
            out[i] = kept[half:].astype(bf16)
        keep[i] = kept[:half] if s else kept

    for r in range(n_z + 2 * stages + 1):
        moves = []
        i = r - stages
        if 0 <= i < n_z:
            far_sib = core_swap(far[i])
        for s in range(stages):
            if 0 <= r - s < n_z:
                i = r - s
                got = stage_swap(blk[i], s)
                if s < stages - 1:
                    moves.append((got, lambda got, i=i: put(blk, i, jnp.concatenate([blk[i], got], axis=0))))
                else:
                    moves.append((got, lambda got, i=i: put(far, i, got)))
                    moves.append((core_swap(blk[i]), lambda got, i=i: put(blk_sib, i, got)))
        for s in range(stages):
            i = r - 2 * stages + s
            if 1 <= i <= n_z:
                i %= n_z
                moves.append((stage_swap(out[i], s), lambda got, i=i, s=s: summed(i, s, got)))
        if r + 1 < n_z:
            moves.append((shift(payload, -near[r + 1]), lambda got, i=r + 1: put(blk, i, got[None, None])))
        i = r - 2 * stages - 1
        if 1 <= i < n_z:
            moves.append((shift(keep[i][0, 0].astype(bf16), near[i]), lambda got, i=i: put(back, i, got.astype(f32))))
        made = []
        i = r - stages
        if 0 <= i < n_z:
            made, weights = run_experts(place, first, blk[i], far[i], blk_sib[i], far_sib, weights, block, i == 0)
        gots = [got for got, _ in moves]
        if r in tied:
            gots, made = lax.optimization_barrier((gots, made))
        for got, (_, take) in zip(gots, moves):
            take(got)
        if made:
            mine_keep, mine_send, sib_keep, sib_send = made
            out[i] = (mine_send.astype(f32) + core_swap(sib_send).astype(f32)).astype(bf16)
            keep[i] = mine_keep.astype(f32) + core_swap(sib_keep).astype(f32)
    return sum([back[i] for i in range(1, n_z)], keep[0][0, 0]).astype(bf16)


def solution(mesh):
    placed = (
        P("expert", "tensor"),
        P("tensor"),
        P("expert", None),
        P("expert", None),
        P("expert", "tensor", None),
        P("expert", "tensor", None),
        P("expert", "tensor", None),
    )
    return jax.shard_map(
        body, mesh=mesh, in_specs=placed, out_specs=P("expert", "tensor"), check_vma=False
    )
```

```python
import functools

import jax
import jax.numpy as jnp
from jax import lax
from jax.experimental import pallas as pl
from jax.experimental.pallas import tpu as pltpu
from jax.sharding import PartitionSpec as P

AXES = ("expert", "tensor")
CORES = 2
LANES = 128
SPLIT = 3
epsilon = 1e-06
NT = (((1,), (1,)), ((), ()))
TN = (((0,), (0,)), ((), ()))
f32 = jnp.float32
bf16 = jnp.bfloat16
VMEM = pl.BlockSpec(memory_space=pltpu.VMEM)


def masks_of(n_tensor):
    first = [1 << b for b in range(n_tensor.bit_length() - 1)]
    return first, first[::-1]


def spread(masks, j):
    out = 0
    for s, m in enumerate(masks):
        if (j >> s) & 1:
            out ^= m
    return out


def mirror(pieces, j):
    first, second = masks_of(pieces)
    return spread([1 << second.index(m) for m in first], j)


def payload_kernel(experts_all, hidden, gain, ids, weights, out):
    block, width = hidden.shape
    h = hidden[...].astype(f32)
    out[0:block, :] = (h * gain[...]).astype(bf16)
    squares = jnp.sum(h * h, axis=1, keepdims=True)
    rows = [jnp.broadcast_to(squares, (block, LANES)).T[0:1, :]]
    for e in range(experts_all):
        rows.append(jnp.sum(jnp.where(ids[...] == e, weights[...], 0.0), axis=0, keepdims=True))
    slots = []
    for v in rows:
        for _ in range(SPLIT):
            part = v.astype(bf16).astype(f32)
            slots.append(part)
            v = v - part
    per_row = width // LANES
    zero = jnp.zeros((1, LANES), f32)
    n_extra = out.shape[0] - block
    slots += [zero] * (n_extra * per_row - len(slots))
    lines = [jnp.concatenate(slots[r * per_row : (r + 1) * per_row], axis=1) for r in range(n_extra)]
    out[block:, :] = jnp.concatenate(lines, axis=0).astype(bf16)


def expert_kernel(pieces, offsets, block, fetch, *refs):
    a0, a1, b0, b1, wg, wu, wd = refs[:7]
    mine_keep, mine_send, sib_keep, sib_send = refs[7:11]
    xs, hs = refs[11 + 3 * fetch : 13 + 3 * fetch]
    half = pieces // 2
    rows = offsets * block
    width = a0.shape[3]
    n_extra = a0.shape[2] - block
    n_exp, hidden = wg.shape[0], wg.shape[1]
    others = [mirror(pieces, j) for j in range(pieces)]
    group_here, slice_here = lax.axis_index("expert"), lax.axis_index("tensor")
    masks = masks_of(pieces)

    def piece(side, j):
        j = others[j] if side else j
        return ((a0, a1), (b0, b1))[side][j // half], j % half

    def columns(j):
        chunk = slice_here ^ jnp.where(group_here % CORES == 0, spread(masks[0], j), spread(masks[1], j))
        return pl.ds(pl.multiple_of(chunk * width, width), width)

    copies = []
    if fetch:
        (wg_from, wu_from, wd_from), (wg, wu, wd), sems = (wg, wu, wd), refs[11:14], refs[-1]
        moves = [(x.at[e], y.at[e]) for e in range(n_exp) for x, y in ((wg_from, wg), (wu_from, wu))]
        moves += [(wd_from.at[:, columns(j)], wd.at[:, columns(j)]) for j in range(pieces)]
        copies = [pltpu.make_async_copy(x, y, sems.at[n]) for n, (x, y) in enumerate(moves)]
        for copy in copies:
            copy.start()

    def wait(n):
        if copies:
            copies[n].wait()

    for side in range(2):
        for j in range(pieces):
            src, i = piece(side, j)
            for o in range(offsets):
                at = side * rows + o * block
                xs[at : at + block, j * width : (j + 1) * width] = src[i, o, 0:block, :]

    value = (
        lax.broadcasted_iota(jnp.int32, (n_extra, width), 0) * (width // LANES)
        + lax.broadcasted_iota(jnp.int32, (n_extra, width), 1) // LANES
    ) // SPLIT

    def pick(table, v):
        row = jnp.sum(jnp.where(value == v, table, 0.0), axis=0, keepdims=True)
        return sum(row[:, g * LANES : (g + 1) * LANES] for g in range(width // LANES))

    scales, picked = [], [[] for _ in range(n_exp)]
    for side in range(2):
        for o in range(offsets):
            tables = []
            for j in range(pieces):
                src, i = piece(side, j)
                tables.append(src[i, o, block:, :].astype(f32))
            scales.append(pick(sum(tables), 0))
            for e in range(n_exp):
                picked[e].append(pick(tables[0], group_here * n_exp + (1 + e)))
    scale = lax.rsqrt(jnp.concatenate(scales, axis=1) / (pieces * width) + epsilon)

    for e in range(n_exp):
        wait(2 * e)
        wait(2 * e + 1)
        gate = jnp.zeros((hidden, 2 * rows), f32)
        up = jnp.zeros((hidden, 2 * rows), f32)
        for j in range(pieces):
            x = xs[:, j * width : (j + 1) * width]
            gate += lax.dot_general(wg[e, :, columns(j)], x, NT, preferred_element_type=f32)
            up += lax.dot_general(wu[e, :, columns(j)], x, NT, preferred_element_type=f32)
        gate = gate * scale
        inner = gate / (1.0 + jnp.exp(-gate)) * (up * scale) * jnp.concatenate(picked[e], axis=1)
        hs[e * hidden : (e + 1) * hidden, :] = inner.astype(bf16)

    for j in range(pieces):
        wait(2 * n_exp + j)
        out = lax.dot_general(hs[...], wd[:, columns(j)], TN, preferred_element_type=f32).astype(bf16)
        for side, (keep, away) in enumerate(((mine_keep, mine_send), (sib_keep, sib_send))):
            to = others[j] if side else j
            for o in range(offsets):
                at = side * rows + o * block
                (keep if to < half else away)[to % half, o] = out[at : at + block]


def run_experts(a0, a1, b0, b1, weights, block, fetch):
    half, offsets, _, width = a0.shape
    pieces = 2 * half
    rows = offsets * block
    n_exp, hidden = weights[0].shape[0], weights[2].shape[0]
    held = [pltpu.VMEM(w.shape, w.dtype) for w in weights] if fetch else []
    sems = [pltpu.SemaphoreType.DMA((2 * n_exp + pieces,))] if fetch else []
    out = pl.pallas_call(
        functools.partial(expert_kernel, pieces, offsets, block, fetch),
        out_shape=[jax.ShapeDtypeStruct((half, offsets, block, width), bf16)] * 4 + held,
        in_specs=[VMEM] * 4 + [pl.BlockSpec(memory_space=pl.ANY) if fetch else VMEM] * 3,
        out_specs=[VMEM] * (4 + len(held)),
        scratch_shapes=[
            pltpu.VMEM((2 * rows, pieces * width), bf16),
            pltpu.VMEM((hidden, 2 * rows), bf16),
        ]
        + sems,
        compiler_params=pltpu.CompilerParams(vmem_limit_bytes=30 * 1024 * 1024),
        cost_estimate=pl.CostEstimate(
            flops=4 * rows * 3 * hidden * pieces * width,
            bytes_accessed=8 * rows * pieces * width,
            transcendentals=2 * rows * hidden,
        ),
    )(a0, a1, b0, b1, *weights)
    if fetch:
        weights = [pltpu.with_memory_space_constraint(w, pltpu.VMEM) for w in out[4:]]
    return list(out[:4]), weights


def body(hidden_in, norm_gain, expert_ids, route_weights, w_gate, w_up, w_down):
    block, width = hidden_in.shape
    exp_local = w_gate.shape[0]
    groups, n_tensor = lax.axis_size("expert"), lax.axis_size("tensor")
    n_z = groups // CORES
    experts_all = exp_local * groups
    masks = masks_of(n_tensor)
    stages = len(masks[0])

    def send(value, target):
        pairs = []
        for z in range(n_z):
            for c in range(CORES):
                for t in range(n_tensor):
                    z2, c2, t2 = target(z, c, t)
                    pairs.append(((z * CORES + c) * n_tensor + t, (z2 * CORES + c2) * n_tensor + t2))
        return lax.ppermute(value, AXES, pairs)

    def stage_swap(value, s):
        return send(value, lambda z, c, t: (z, c, t ^ masks[c][s]))

    def core_swap(value):
        return send(value, lambda z, c, t: (z, 1 - c, t))

    def shift(value, k):
        return send(value, lambda z, c, t: ((z + k) % n_z, c, t)) if k % n_z else value

    slots = SPLIT * (1 + experts_all)
    n_extra = -(-slots // (8 * width // LANES)) * 8
    payload = pl.pallas_call(
        functools.partial(payload_kernel, experts_all),
        out_shape=jax.ShapeDtypeStruct((block + n_extra, width), bf16),
        in_specs=[VMEM] * 4,
        out_specs=VMEM,
    )(hidden_in, norm_gain[None, :], expert_ids.T, route_weights.T)

    weights = [w_gate, w_up, w_down.reshape(-1, w_down.shape[2])]

    blk, far, blk_sib, out, keep, back = {0: payload[None, None]}, {}, {}, {}, {}, {}
    passing, still = payload, []
    tied = range(2, n_z + stages)

    def put(store, i, value):
        store[i] = value

    def summed(i, s, got):
        kept = keep[i] + got.astype(f32)
        half = kept.shape[0] // 2
        if s:
            out[i] = kept[half:].astype(bf16)
        keep[i] = kept[:half] if s else kept

    for r in range(n_z + 2 * stages + 1):
        short = []
        moves = [
            (core_swap(sib_keep), lambda got, i=i: put(keep, i, keep[i] + got.astype(f32))) for i, sib_keep in still
        ]
        still = []
        ready = [r - stages] if 1 <= r - stages < n_z else []
        if r == stages + 2:
            ready.append(0)
        far_sib = [core_swap(far[i]) for i in ready]
        for s in range(stages):
            i = r - s
            if 0 <= i < n_z:
                got = stage_swap(blk[i], s)
                if s < stages - 1:
                    widen = lambda got, i=i: put(blk, i, jnp.concatenate([blk[i], got], axis=0))
                    (moves if s else short).append((got, widen))
                else:
                    moves.append((got, lambda got, i=i: put(far, i, got)))
                    moves.append((core_swap(blk[i]), lambda got, i=i: put(blk_sib, i, got)))
        for s in range(stages):
            i = r - 2 * stages + s
            if 1 <= i <= n_z:
                i %= n_z
                fold = lambda got, i=i, s=s: summed(i, s, got)
                (moves if s else short).append((stage_swap(out[i], s), fold))
        if r + 1 < n_z:
            moves.append((shift(passing, -1), lambda got, i=r + 1: put(blk, i, got[None, None])))
            passing = moves[-1][0]
        i = r - 2 * stages - 1
        if 1 <= i < n_z:
            done = keep[i][0, 0]
            if i > n_z // 2:
                done = done + back.pop(i - 1)
            done = shift(done.astype(bf16), -1 if 2 * i >= n_z else i)
            moves.append((done, lambda got, i=i: put(back, i, got.astype(f32))))
        made = []
        for i, sib in zip(ready, far_sib):
            parts, weights = run_experts(blk[i], far[i], blk_sib[i], sib, weights, block, r == stages + 1)
            made.append(parts)
        moves = short + moves
        gots = [got for got, _ in moves]
        if made:
            away = [parts[3] for parts in made]
            gots[: len(short)], away = lax.optimization_barrier((gots[: len(short)], away))
            made = [parts[:3] + [sib] for parts, sib in zip(made, away)]
        if r == n_z + stages:
            gots[: len(short)], out[0] = lax.optimization_barrier((gots[: len(short)], out[0]))
        if r in tied:
            firm = [parts[:3] for parts in made]
            gots, firm, far[0] = lax.optimization_barrier((gots, firm, far.get(0)))
            made = [kept + parts[3:] for kept, parts in zip(firm, made)]
        for got, (_, take) in zip(gots, moves):
            take(got)
        for i, (mine_keep, mine_send, sib_keep, sib_send) in zip(ready, made):
            out[i] = (mine_send.astype(f32) + core_swap(sib_send).astype(f32)).astype(bf16)
            keep[i] = mine_keep.astype(f32)
            still.append((i, sib_keep))
    return sum(back.values(), keep[0][0, 0]).astype(bf16)


def solution(mesh):
    placed = (
        P("expert", "tensor"),
        P("tensor"),
        P("expert", None),
        P("expert", None),
        P("expert", "tensor", None),
        P("expert", "tensor", None),
        P("expert", "tensor", None),
    )
    return jax.shard_map(
        body, mesh=mesh, in_specs=placed, out_specs=P("expert", "tensor"), check_vma=False
    )
```

```python
import functools

import jax
import jax.numpy as jnp
from jax import lax
from jax.experimental import pallas as pl
from jax.experimental.pallas import tpu as pltpu
from jax.sharding import PartitionSpec as P

AXES = ("expert", "tensor")
CORES = 2
LANES = 128
SPLIT = 3
epsilon = 1e-06
NT = (((1,), (1,)), ((), ()))
TN = (((0,), (0,)), ((), ()))
f32 = jnp.float32
bf16 = jnp.bfloat16
VMEM = pl.BlockSpec(memory_space=pltpu.VMEM)


def masks_of(n_tensor):
    first = [1 << b for b in range(n_tensor.bit_length() - 1)]
    return first, first[::-1]


def spread(masks, j):
    out = 0
    for s, m in enumerate(masks):
        if (j >> s) & 1:
            out ^= m
    return out


def mirror(pieces, j):
    first, second = masks_of(pieces)
    return spread([1 << second.index(m) for m in first], j)


def payload_kernel(experts_all, hidden, gain, ids, weights, out):
    block, width = hidden.shape
    h = hidden[...].astype(f32)
    out[0:block, :] = (h * gain[...]).astype(bf16)
    squares = jnp.sum(h * h, axis=1, keepdims=True)
    rows = [jnp.broadcast_to(squares, (block, LANES)).T[0:1, :]]
    for e in range(experts_all):
        rows.append(jnp.sum(jnp.where(ids[...] == e, weights[...], 0.0), axis=0, keepdims=True))
    slots = []
    for v in rows:
        for _ in range(SPLIT):
            part = v.astype(bf16).astype(f32)
            slots.append(part)
            v = v - part
    per_row = width // LANES
    zero = jnp.zeros((1, LANES), f32)
    n_extra = out.shape[0] - block
    slots += [zero] * (n_extra * per_row - len(slots))
    lines = [jnp.concatenate(slots[r * per_row : (r + 1) * per_row], axis=1) for r in range(n_extra)]
    out[block:, :] = jnp.concatenate(lines, axis=0).astype(bf16)


def expert_kernel(pieces, offsets, block, fetch, *refs):
    a0, a1, b0, b1, wg, wu, wd = refs[:7]
    mine_keep, mine_send, sib_keep, sib_send = refs[7:11]
    xs, hs = refs[11 + 3 * fetch : 13 + 3 * fetch]
    half = pieces // 2
    rows = offsets * block
    width = a0.shape[3]
    n_extra = a0.shape[2] - block
    n_exp, hidden = wg.shape[0], wg.shape[1]
    others = [mirror(pieces, j) for j in range(pieces)]
    group_here, slice_here = lax.axis_index("expert"), lax.axis_index("tensor")
    masks = masks_of(pieces)

    def piece(side, j):
        j = others[j] if side else j
        return ((a0, a1), (b0, b1))[side][j // half], j % half

    def columns(j):
        chunk = slice_here ^ jnp.where(group_here % CORES == 0, spread(masks[0], j), spread(masks[1], j))
        return pl.ds(pl.multiple_of(chunk * width, width), width)

    copies = []
    if fetch:
        (wg_from, wu_from, wd_from), (wg, wu, wd), sems = (wg, wu, wd), refs[11:14], refs[-1]
        moves = [(x.at[e], y.at[e]) for e in range(n_exp) for x, y in ((wg_from, wg), (wu_from, wu))]
        moves += [(wd_from.at[:, columns(j)], wd.at[:, columns(j)]) for j in range(pieces)]
        copies = [pltpu.make_async_copy(x, y, sems.at[n]) for n, (x, y) in enumerate(moves)]
        for copy in copies:
            copy.start()

    def wait(n):
        if copies:
            copies[n].wait()

    for side in range(2):
        for j in range(pieces):
            src, i = piece(side, j)
            for o in range(offsets):
                at = side * rows + o * block
                xs[at : at + block, j * width : (j + 1) * width] = src[i, o, 0:block, :]

    value = (
        lax.broadcasted_iota(jnp.int32, (n_extra, width), 0) * (width // LANES)
        + lax.broadcasted_iota(jnp.int32, (n_extra, width), 1) // LANES
    ) // SPLIT

    def pick(table, v):
        row = jnp.sum(jnp.where(value == v, table, 0.0), axis=0, keepdims=True)
        return sum(row[:, g * LANES : (g + 1) * LANES] for g in range(width // LANES))

    scales, picked = [], [[] for _ in range(n_exp)]
    for side in range(2):
        for o in range(offsets):
            tables = []
            for j in range(pieces):
                src, i = piece(side, j)
                tables.append(src[i, o, block:, :].astype(f32))
            scales.append(pick(sum(tables), 0))
            for e in range(n_exp):
                picked[e].append(pick(tables[0], group_here * n_exp + (1 + e)))
    scale = lax.rsqrt(jnp.concatenate(scales, axis=1) / (pieces * width) + epsilon)

    for e in range(n_exp):
        wait(2 * e)
        wait(2 * e + 1)
        gate = jnp.zeros((hidden, 2 * rows), f32)
        up = jnp.zeros((hidden, 2 * rows), f32)
        for j in range(pieces):
            x = xs[:, j * width : (j + 1) * width]
            gate += lax.dot_general(wg[e, :, columns(j)], x, NT, preferred_element_type=f32)
            up += lax.dot_general(wu[e, :, columns(j)], x, NT, preferred_element_type=f32)
        gate = gate * scale
        inner = gate / (1.0 + jnp.exp(-gate)) * (up * scale) * jnp.concatenate(picked[e], axis=1)
        hs[e * hidden : (e + 1) * hidden, :] = inner.astype(bf16)

    for j in range(pieces):
        wait(2 * n_exp + j)
        out = lax.dot_general(hs[...], wd[:, columns(j)], TN, preferred_element_type=f32).astype(bf16)
        for side, (keep, away) in enumerate(((mine_keep, mine_send), (sib_keep, sib_send))):
            to = others[j] if side else j
            for o in range(offsets):
                at = side * rows + o * block
                (keep if to < half else away)[to % half, o] = out[at : at + block]


def run_experts(a0, a1, b0, b1, weights, block, fetch):
    half, offsets, _, width = a0.shape
    pieces = 2 * half
    rows = offsets * block
    n_exp, hidden = weights[0].shape[0], weights[2].shape[0]
    held = [pltpu.VMEM(w.shape, w.dtype) for w in weights] if fetch else []
    sems = [pltpu.SemaphoreType.DMA((2 * n_exp + pieces,))] if fetch else []
    out = pl.pallas_call(
        functools.partial(expert_kernel, pieces, offsets, block, fetch),
        out_shape=[jax.ShapeDtypeStruct((half, offsets, block, width), bf16)] * 4 + held,
        in_specs=[VMEM] * 4 + [pl.BlockSpec(memory_space=pl.ANY) if fetch else VMEM] * 3,
        out_specs=[VMEM] * (4 + len(held)),
        scratch_shapes=[
            pltpu.VMEM((2 * rows, pieces * width), bf16),
            pltpu.VMEM((hidden, 2 * rows), bf16),
        ]
        + sems,
        compiler_params=pltpu.CompilerParams(vmem_limit_bytes=30 * 1024 * 1024),
        cost_estimate=pl.CostEstimate(
            flops=4 * rows * 3 * hidden * pieces * width,
            bytes_accessed=8 * rows * pieces * width,
            transcendentals=2 * rows * hidden,
        ),
    )(a0, a1, b0, b1, *weights)
    if fetch:
        weights = [pltpu.with_memory_space_constraint(w, pltpu.VMEM) for w in out[4:]]
    return list(out[:4]), weights


def body(hidden_in, norm_gain, expert_ids, route_weights, w_gate, w_up, w_down):
    block, width = hidden_in.shape
    exp_local = w_gate.shape[0]
    groups, n_tensor = lax.axis_size("expert"), lax.axis_size("tensor")
    n_z = groups // CORES
    experts_all = exp_local * groups
    masks = masks_of(n_tensor)
    stages = len(masks[0])

    def send(value, target):
        pairs = []
        for z in range(n_z):
            for c in range(CORES):
                for t in range(n_tensor):
                    z2, c2, t2 = target(z, c, t)
                    pairs.append(((z * CORES + c) * n_tensor + t, (z2 * CORES + c2) * n_tensor + t2))
        return lax.ppermute(value, AXES, pairs)

    def stage_swap(value, s):
        return send(value, lambda z, c, t: (z, c, t ^ masks[c][s]))

    def core_swap(value):
        return send(value, lambda z, c, t: (z, 1 - c, t))

    def shift(value, k):
        return send(value, lambda z, c, t: ((z + k) % n_z, c, t)) if k % n_z else value

    slots = SPLIT * (1 + experts_all)
    n_extra = -(-slots // (8 * width // LANES)) * 8
    payload = pl.pallas_call(
        functools.partial(payload_kernel, experts_all),
        out_shape=jax.ShapeDtypeStruct((block + n_extra, width), bf16),
        in_specs=[VMEM] * 4,
        out_specs=VMEM,
    )(hidden_in, norm_gain[None, :], expert_ids.T, route_weights.T)

    weights = [w_gate, w_up, w_down.reshape(-1, w_down.shape[2])]

    blk, far, blk_sib, out, keep, back = {0: payload[None, None]}, {}, {}, {}, {}, {}
    passing, still = payload, []
    tied = range(2, n_z + stages)

    def put(store, i, value):
        store[i] = value

    def summed(i, s, got):
        kept = keep[i] + got.astype(f32)
        half = kept.shape[0] // 2
        if s:
            out[i] = kept[half:].astype(bf16)
        keep[i] = kept[:half] if s else kept

    for r in range(n_z + 2 * stages + 1):
        short = []
        moves = [
            (core_swap(sib_keep), lambda got, i=i: put(keep, i, keep[i] + got.astype(f32))) for i, sib_keep in still
        ]
        still = []
        ready = [r - stages] if 1 <= r - stages < n_z else []
        if r == stages + 2:
            ready.append(0)
        far_sib = [core_swap(far[i]) for i in ready]
        for s in range(stages):
            i = r - s
            if 0 <= i < n_z:
                got = stage_swap(blk[i], s)
                if s < stages - 1:
                    widen = lambda got, i=i: put(blk, i, jnp.concatenate([blk[i], got], axis=0))
                    (moves if s else short).append((got, widen))
                else:
                    moves.append((got, lambda got, i=i: put(far, i, got)))
                    moves.append((core_swap(blk[i]), lambda got, i=i: put(blk_sib, i, got)))
        for s in range(stages):
            i = r - 2 * stages + s
            if 1 <= i <= n_z:
                i %= n_z
                fold = lambda got, i=i, s=s: summed(i, s, got)
                (moves if s else short).append((stage_swap(out[i], s), fold))
        if r + 1 < n_z:
            moves.append((shift(passing, -1), lambda got, i=r + 1: put(blk, i, got[None, None])))
            passing = moves[-1][0]
        i = r - 2 * stages - 1
        if 1 <= i < n_z:
            done = keep[i][0, 0]
            done = shift(done.astype(bf16), i)
            moves.append((done, lambda got, i=i: put(back, i, got.astype(f32))))
        made = []
        for i, sib in zip(ready, far_sib):
            parts, weights = run_experts(blk[i], far[i], blk_sib[i], sib, weights, block, r == stages + 1)
            made.append(parts)
        moves = short + moves
        gots = [got for got, _ in moves]
        if made:
            away = [parts[3] for parts in made]
            gots[: len(short)], away = lax.optimization_barrier((gots[: len(short)], away))
            made = [parts[:3] + [sib] for parts, sib in zip(made, away)]
        if r == n_z + stages:
            gots[: len(short)], out[0] = lax.optimization_barrier((gots[: len(short)], out[0]))
        if r in tied:
            firm = [parts[:3] for parts in made]
            gots, firm, far[0] = lax.optimization_barrier((gots, firm, far.get(0)))
            made = [kept + parts[3:] for kept, parts in zip(firm, made)]
        for got, (_, take) in zip(gots, moves):
            take(got)
        for i, (mine_keep, mine_send, sib_keep, sib_send) in zip(ready, made):
            out[i] = (mine_send.astype(f32) + core_swap(sib_send).astype(f32)).astype(bf16)
            keep[i] = mine_keep.astype(f32)
            still.append((i, sib_keep))
    return sum(back.values(), keep[0][0, 0]).astype(bf16)


def solution(mesh):
    placed = (
        P("expert", "tensor"),
        P("tensor"),
        P("expert", None),
        P("expert", None),
        P("expert", "tensor", None),
        P("expert", "tensor", None),
        P("expert", "tensor", None),
    )
    return jax.shard_map(
        body, mesh=mesh, in_specs=placed, out_specs=P("expert", "tensor"), check_vma=False
    )
```
